32 devices in a mesh: groups: 2 (over x), tensor: 8 (over z, y), seq: 2 (over core).
Axes of the slice: x: 2, y: 2, z: 4, core: 2. Of those that a mesh axis runs over, the one named last changes fastest.
Arguments:
- token_input_rows: bfloat16 [1024, 8192], P(('groups', 'tensor', 'seq')), parts along dimension 0, may hold values from -6 to 6
- base_projection_weight: bfloat16 [8192, 16384], P(None, 'tensor'), may hold values from -0.0625 to 0.0625
- adapter_down_maps: bfloat16 [8, 8192, 64], P('tensor'), may hold values from -0.0625 to 0.0625
- adapter_up_maps: bfloat16 [8, 64, 16384], P('tensor'), may hold values from -0.75 to 0.75
- token_adapter_index: int32 [1024], P(('groups', 'tensor', 'seq')), parts along dimension 0, may hold values from 0 to 7, as said below
- adapter_slot_table: int32 [8], replicated, may hold values from 0 to 7, each once
Outputs:
- projected: bfloat16 [1024, 16384], P(('groups', 'tensor', 'seq')), parts along dimension 0
The draws below stay inside these ranges and needn't reach their ends.
There are 2 independent parts, one for each index of `groups`. The reference program is written for one: setup_inputs(seed, part) draws one part's arguments, and reference() takes and returns one part's arrays. A program takes and returns all parts, laid end to end along the dimension named above; an argument that names none is the same for every part. Nothing has to cross between parts.
Inputs may be any that keep to these rules, and one draw needn't show every extreme that they name: `token_adapter_index`: in each aligned block of 32 tokens (the tokens of one device) every adapter is named at most 5 times; one adapter, the same in every block, is named exactly 5 times in every block. `adapter_slot_table`: each slot is named by exactly one adapter.
All inputs are finite; a program needn't handle non-finite values.
Results may differ from the reference program's by a relative error of at most 0.0057.
Values may be sent and summed in bfloat16 or wider, within the bound.
No kernel may reach another device: no remote copies, remote signals or barrier semaphores. Data moves between devices by JAX's collectives and lax.ppermute only.
A program may use at most 128 MiB of HBM per device.

```python
import jax
import jax.numpy as jnp
from jax import lax

MODEL_WIDTH = 8192
OUTPUT_UNITS = 16384
ADAPTER_RANK = 64
TOK_DEV = 32
TOKEN_COUNT = 512
ADAPTER_COUNT = 8
CAP = 5


def draw_token_adapter_index(key, part):
    key = jax.random.fold_in(key, 11)
    blocks = TOKEN_COUNT // TOK_DEV
    hottest = jax.random.randint(jax.random.fold_in(key, 1), (), 0, ADAPTER_COUNT)
    slot_pool = jnp.arange(ADAPTER_COUNT * CAP, dtype=jnp.int32) // CAP
    block_keys = jax.random.split(jax.random.fold_in(key, 2), blocks)

    def draw_block(block_key):
        shuffle_key, order_key = jax.random.split(block_key)
        shuffled_order = jax.random.permutation(shuffle_key, ADAPTER_COUNT * CAP)
        shuffled = slot_pool[shuffled_order]
        priority = jnp.where(shuffled == hottest, 0, 1) * (ADAPTER_COUNT * CAP) + jnp.arange(ADAPTER_COUNT * CAP, dtype=jnp.int32)
        chosen = shuffled[jnp.argsort(priority)][:TOK_DEV]
        return chosen[jax.random.permutation(order_key, TOK_DEV)]
    return jax.vmap(draw_block)(block_keys).reshape(TOKEN_COUNT).astype(jnp.int32)


def block_scale(own_key, shape, pieces, low, top_value):
    level, own = 1.0, jax.random.fold_in(own_key, 6)
    for axis_at, shards_of in pieces:
        steps = jnp.exp(jax.random.uniform(jax.random.fold_in(own, axis_at), (shards_of,), jnp.float32, low / len(pieces), top_value / len(pieces)))
        level = level * jnp.repeat(steps, shape[axis_at] // shards_of).reshape([-1 if axis == axis_at else 1 for axis in range(len(shape))])
    return level


def centred(stream_key, shape, spread, reach, shards=(), kind=jnp.bfloat16):
    drawn = jax.random.normal(stream_key, shape, jnp.float32) * spread
    if len(shards) > 0:
        drawn = block_scale(stream_key, shape, shards, -0.22, 0.18) * drawn
    return jnp.clip(drawn, min=-reach, max=reach).astype(kind)


def setup_inputs(seed: int = 0, part: int = 0) -> dict:
    seeds = jax.random.split(jax.random.key(seed), 7)
    part_splits = jax.random.split(jax.random.fold_in(seeds[6], part), 7)
    token_input_rows = centred(part_splits[0], (TOKEN_COUNT, MODEL_WIDTH), 1.0, 6.0, ((0, 16),))
    base_projection_weight = centred(seeds[1], (MODEL_WIDTH, OUTPUT_UNITS), MODEL_WIDTH ** -0.5, 0.0625, ((1, 8),))
    adapter_down_maps = centred(seeds[2], (ADAPTER_COUNT, MODEL_WIDTH, ADAPTER_RANK), MODEL_WIDTH ** -0.5, 0.0625, ((0, 8),))
    adapter_up_maps = centred(seeds[3], (ADAPTER_COUNT, ADAPTER_RANK, OUTPUT_UNITS), ADAPTER_RANK ** -0.5, 0.75, ((0, 8),))
    token_adapter_index = draw_token_adapter_index(jax.random.fold_in(jax.random.fold_in(seeds[6], part), 71), part)
    adapter_slot_table = jax.random.permutation(seeds[5], ADAPTER_COUNT).astype(jnp.int32)
    return dict(token_input_rows=token_input_rows, base_projection_weight=base_projection_weight, adapter_down_maps=adapter_down_maps, adapter_up_maps=adapter_up_maps, token_adapter_index=token_adapter_index, adapter_slot_table=adapter_slot_table)


def reference(token_input_rows, base_projection_weight, adapter_down_maps, adapter_up_maps, token_adapter_index, adapter_slot_table):
    base_output = jnp.dot(token_input_rows, base_projection_weight, preferred_element_type=jnp.float32).astype(jnp.bfloat16)
    slot_index = adapter_slot_table[token_adapter_index].astype(jnp.int32)
    blocks = TOKEN_COUNT // TOK_DEV
    grouped_inputs = token_input_rows.reshape(blocks, TOK_DEV, MODEL_WIDTH)
    grouped_slot_index = slot_index.reshape(blocks, TOK_DEV)

    def block_update(packed):
        block_rows, block_slot_index = packed
        selected_down_maps = adapter_down_maps[block_slot_index].astype(jnp.float32)
        rank_activations = jnp.einsum("td,tdr->tr", block_rows.astype(jnp.float32), selected_down_maps).astype(jnp.bfloat16)
        selected_up_maps = adapter_up_maps[block_slot_index].astype(jnp.float32)
        return jnp.einsum("ja,jaz->jz", rank_activations.astype(jnp.float32), selected_up_maps).astype(jnp.bfloat16)

    adapter_update = lax.map(block_update, (grouped_inputs, grouped_slot_index)).reshape(TOKEN_COUNT, OUTPUT_UNITS)
    return (base_output.astype(jnp.float32) + adapter_update.astype(jnp.float32)).astype(jnp.bfloat16)
```

```python
import functools

import jax
import jax.numpy as jnp
from jax import lax
from jax.experimental import pallas as pl
from jax.experimental.pallas import tpu as pltpu
from jax.sharding import PartitionSpec as P

BF16 = jnp.bfloat16
F32 = jnp.float32
ANY = pl.BlockSpec(memory_space=pl.ANY)
VMEM = pl.BlockSpec(memory_space=pltpu.VMEM)
SMEM = pl.BlockSpec(memory_space=pltpu.SMEM)


def ring_order(count):
    if count % 2 or count > 8:
        return list(range(count))
    return list(range(0, count, 2)) + list(range(1, count, 2))[::-1]


def fetch_rows(units, place, rows, held, sem):
    return [
        pltpu.make_async_copy(
            unit, held.at[pl.ds(pl.multiple_of(place[j] * rows, rows), rows)], sem.at[j]
        )
        for j, unit in enumerate(units)
    ]


def rank_kernel(count, rows, *refs):
    place, mine = refs[:2]
    units = refs[2 : 2 + count]
    down, slots, out, held, sem = refs[2 + count :]
    copies = fetch_rows(units, place, rows, held, sem)
    for copy in copies:
        copy.start()
    for copy in copies:
        copy.wait()
    low = jnp.dot(held[...], down[...], preferred_element_type=F32)
    out[...] = jnp.where(slots[...] == mine[0], low, 0.0).astype(BF16)


def rank_rows(units, place, mine, down, slots):
    count, rows = len(units), units[0].shape[0]
    width, rank = down.shape
    return pl.pallas_call(
        functools.partial(rank_kernel, count, rows),
        in_specs=[SMEM, SMEM] + [ANY] * count + [VMEM, VMEM],
        out_specs=VMEM,
        out_shape=jax.ShapeDtypeStruct((count * rows, rank), BF16),
        scratch_shapes=[
            pltpu.VMEM((count * rows, width), BF16),
            pltpu.SemaphoreType.DMA((count,)),
        ],
        compiler_params=pltpu.CompilerParams(vmem_limit_bytes=28 << 20),
        cost_estimate=pl.CostEstimate(
            flops=2 * count * rows * width * rank,
            bytes_accessed=2 * width * (count * rows + rank),
            transcendentals=0,
        ),
    )(place, mine, *units, down, slots)


def project_kernel(count, rows, quarters, *refs):
    place, quarter_of = refs[:2]
    units = refs[2 : 2 + count]
    weight = refs[2 + count]
    ups = refs[3 + count : 3 + count + quarters]
    low, slots, out, held, w_held, u_held, x_sem, w_sem, u_sem = refs[3 + count + quarters :]
    columns = weight.shape[1]
    pieces = w_sem.shape[0]
    step = columns // pieces
    rank = low.shape[1]
    per = u_held.shape[0] // quarters
    sub = rank // quarters

    def weight_copy(i):
        at = pl.ds(i * step, step)
        return pltpu.make_async_copy(weight.at[:, at], w_held.at[i], w_sem.at[i])

    x_copies = fetch_rows(units, place, rows, held, x_sem)
    for copy in x_copies:
        copy.start()
    for i in range(pieces):
        weight_copy(i).start()
    u_copies = [
        pltpu.make_async_copy(
            up, u_held.at[pl.ds(pl.multiple_of(quarter_of[j] * per, per), per)], u_sem.at[j]
        )
        for j, up in enumerate(ups)
    ]
    for copy in u_copies:
        copy.start()
    depth = u_held.shape[0]
    at = lax.broadcasted_iota(jnp.int32, (rank, depth), 1)
    entry = lax.broadcasted_iota(jnp.int32, (rank, depth), 0)
    spread = jnp.where(entry == at // per * sub + at % sub, 1.0, 0.0).astype(BF16)
    wide = jnp.dot(low[...], spread, preferred_element_type=F32)
    owner = lax.broadcasted_iota(jnp.int32, wide.shape, 1) % per // sub
    wide = jnp.where(owner == slots[...], wide, 0.0).astype(BF16)
    for copy in x_copies:
        copy.wait()
    for copy in u_copies:
        copy.wait()
    for i in range(pieces):
        cols = slice(i * step, (i + 1) * step)
        weight_copy(i).wait()
        base = jnp.dot(held[...], w_held[i], preferred_element_type=F32).astype(BF16)
        delta = jnp.dot(wide, u_held[:, cols], preferred_element_type=F32).astype(BF16)
        out[:, cols] = (base.astype(F32) + delta.astype(F32)).astype(BF16)


def project(units, place, weight, ups, quarter_of, low, slots):
    count, rows = len(units), units[0].shape[0]
    width, columns = weight.shape
    quarters = len(ups)
    depth = sum(u.shape[0] for u in ups)
    pieces = max(1, columns // 256)
    total = count * rows
    return pl.pallas_call(
        functools.partial(project_kernel, count, rows, quarters),
        in_specs=[SMEM, SMEM] + [ANY] * (count + 1 + quarters) + [VMEM, VMEM],
        out_specs=VMEM,
        out_shape=jax.ShapeDtypeStruct((total, columns), BF16),
        scratch_shapes=[
            pltpu.VMEM((total, width), BF16),
            pltpu.VMEM((pieces, width, columns // pieces), BF16),
            pltpu.VMEM((depth, columns), BF16),
            pltpu.SemaphoreType.DMA((count,)),
            pltpu.SemaphoreType.DMA((pieces,)),
            pltpu.SemaphoreType.DMA((quarters,)),
        ],
        compiler_params=pltpu.CompilerParams(vmem_limit_bytes=48 << 20),
        cost_estimate=pl.CostEstimate(
            flops=2 * total * width * columns,
            bytes_accessed=2 * width * (columns + total),
            transcendentals=0,
        ),
    )(place, quarter_of, *units, weight, *ups, low, slots)


def body(
    token_input_rows,
    base_projection_weight,
    adapter_down_maps,
    adapter_up_maps,
    token_adapter_index,
    adapter_slot_table,
):
    count = lax.axis_size("tensor")
    groups, seqs = lax.axis_size("groups"), lax.axis_size("seq")
    me = lax.axis_index("tensor")
    replica = lax.axis_index("groups") * seqs + lax.axis_index("seq")
    rows, width = token_input_rows.shape
    half = rows // 2
    columns = base_projection_weight.shape[1]
    rank = adapter_up_maps.shape[1]

    order = ring_order(count)
    place_of = [order.index(t) for t in range(count)]
    ahead = [(order[p], order[(p + 1) % count]) for p in range(count)]
    behind = [(b, a) for a, b in ahead]

    far = count // 2
    first, second = token_input_rows[:half], token_input_rows[half:]
    chains = [[[first], [first]], [[second], [second]]]
    for k in range(1, far + 1):
        for h in range(2):
            for way, pairs in enumerate((ahead, behind)):
                if k < far or way == h:
                    chains[h][way].append(lax.ppermute(chains[h][way][-1], "tensor", pairs))
    units = []
    for h in range(2):
        held = [chains[h][0][0]]
        for k in range(1, far + 1):
            held += [chains[h][way][k] for way in range(2) if k < len(chains[h][way])]
        units.append(held)
    position = jnp.asarray(place_of, jnp.int32)[me]
    order_array = jnp.asarray(order, jnp.int32)

    def offsets(h):
        found = [0]
        for k in range(1, far + 1):
            found += [(-k, k)[way] for way in range(2) if k < len(chains[h][way])]
        return jnp.asarray(found, jnp.int32)

    places = [order_array[(position + offsets(h)) % count] for h in range(2)]

    replicas = groups * seqs
    sub = rank // replicas
    share = lax.dynamic_slice_in_dim(adapter_up_maps[0], replica * sub, sub, 0)
    share = share.reshape(sub, count, columns).transpose(1, 0, 2)
    share = lax.all_to_all(share, "tensor", split_axis=0, concat_axis=0, tiled=True)
    ups = [share.reshape(count * sub, columns)]
    bit = 1
    while bit < replicas:
        axis, size, flip = ("seq", seqs, bit) if bit < seqs else ("groups", groups, bit // seqs)
        pairs = [(i, i ^ flip) for i in range(size)]
        ups += [lax.ppermute(u, axis, pairs) for u in ups]
        bit *= 2
    quarter_of = replica ^ jnp.arange(replicas, dtype=jnp.int32)

    indices = lax.all_gather(token_adapter_index, "tensor", axis=0, tiled=False)
    matches = indices[:, :, None] == jnp.arange(count, dtype=jnp.int32)
    slots = jnp.sum(jnp.where(matches, adapter_slot_table, 0), axis=2)
    slots = [slots[:, :half].reshape(-1, 1), slots[:, half:].reshape(-1, 1)]

    parts = []
    for h in range(2):
        low = rank_rows(
            units[h], places[h], me.astype(jnp.int32)[None], adapter_down_maps[0], slots[h]
        )
        bit = 1
        while bit < count:
            low = low + lax.ppermute(low, "tensor", [(t, t ^ bit) for t in range(count)])
            bit *= 2
        result = project(
            units[h], places[h], base_projection_weight, ups, quarter_of, low, slots[h]
        )
        parts.append(
            lax.all_to_all(
                result.reshape(count, half, columns), "tensor", split_axis=0, concat_axis=0, tiled=True
            )
        )
    parts = [p.transpose(1, 0, 2).reshape(half, -1) for p in parts]
    return jnp.concatenate(parts, axis=0)


def solution(mesh):
    placed = (
        P(("groups", "tensor", "seq"), None),
        P(None, "tensor"),
        P("tensor", None, None),
        P("tensor", None, None),
        P(("groups", "tensor", "seq")),
        P(),
    )
    return jax.shard_map(
        body,
        mesh=mesh,
        in_specs=placed,
        out_specs=P(("groups", "tensor", "seq"), None),
        check_vma=False,
    )
```

```python
import functools

import jax
import jax.numpy as jnp
from jax import lax
from jax.experimental import pallas as pl
from jax.experimental.pallas import tpu as pltpu
from jax.sharding import PartitionSpec as P

BF16 = jnp.bfloat16
F32 = jnp.float32
HBM = pl.BlockSpec(memory_space=pltpu.HBM)
SMEM = pl.BlockSpec(memory_space=pltpu.SMEM)
LANES = 128


def walks_back(count):
    return count % 2 == 0 and count <= 8


def ring_order(count):
    if walks_back(count):
        return list(range(0, count, 2)) + list(range(1, count, 2))[::-1]
    return list(range(count))


def owner_at(me, offset, count):
    if not walks_back(count):
        return lax.rem(me + offset + count, count)
    place = jnp.where(me % 2 == 0, me // 2, count - 1 - me // 2)
    place = lax.rem(place + offset + count, count)
    return jnp.where(place < count // 2, 2 * place, 2 * (count - 1 - place) + 1)


def fetch_rows(units, held, sem):
    rows = units[0].shape[0]
    return [
        pltpu.make_async_copy(unit, held.at[pl.ds(j * rows, rows)], sem.at[j])
        for j, unit in enumerate(units)
    ]


def row_of(me, place, count, rows):
    offset, part, parts = place
    return pl.multiple_of((owner_at(me, offset, count) * parts + part) * rows, rows)


def start_all(copies):
    for copy in copies:
        copy.start()


def wait_all(copies):
    for copy in copies:
        copy.wait()


def call(kernel, outs, in_specs, scratch, flops, moved):
    return pl.pallas_call(
        kernel,
        in_specs=in_specs,
        out_specs=[HBM] * len(outs),
        out_shape=[jax.ShapeDtypeStruct(out, BF16) for out in outs],
        scratch_shapes=scratch,
        compiler_params=pltpu.CompilerParams(vmem_limit_bytes=60 << 20),
        cost_estimate=pl.CostEstimate(flops=flops, bytes_accessed=moved, transcendentals=0),
    )


def masked_ranks(me, held, d_held):
    width, rank = d_held.shape
    low = jnp.dot(held[:, :width], d_held[...], preferred_element_type=F32)
    low = jnp.where(held[:, width : width + rank].astype(F32) == me.astype(F32), low, 0.0)
    return jnp.concatenate([low, jnp.zeros_like(low)], axis=1).astype(BF16)


def early_rows(ids, units, weight, down):
    fetched, rows = len(units), units[0].shape[0]
    wide = units[0].shape[1]
    columns = weight.shape[1]
    width, rank = down.shape
    total = fetched * rows
    step = min(512, columns)
    pieces = columns // step

    def kernel(ids, *refs):
        units, refs = refs[:fetched], refs[fetched:]
        weight, down, out, low, held, w_held, d_held, o_held, l_held, sem, w_sem, d_sem, o_sem = refs
        copies = fetch_rows(units, held, sem) + [pltpu.make_async_copy(down, d_held, d_sem)]
        w_copies, o_copies = [], []
        for i in range(pieces):
            at = pl.ds(i * step, step)
            w_copies.append(pltpu.make_async_copy(weight.at[:, at], w_held.at[i], w_sem.at[i]))
            o_copies.append(pltpu.make_async_copy(o_held.at[:, at], out.at[:, at], o_sem.at[i]))
        o_copies.append(pltpu.make_async_copy(l_held, low, o_sem.at[pieces]))
        start_all(copies)
        start_all(w_copies)
        wait_all(copies)
        l_held[...] = masked_ranks(ids[0], held, d_held)
        o_copies[pieces].start()
        for i in range(pieces):
            w_copies[i].wait()
            o_held[:, i * step : (i + 1) * step] = jnp.dot(
                held[:, :width], w_held[i], preferred_element_type=F32
            ).astype(BF16)
            o_copies[i].start()
        wait_all(o_copies)

    return call(
        kernel,
        [(total, columns), (total, 2 * rank)],
        [SMEM] + [HBM] * (fetched + 2),
        [
            pltpu.VMEM((total, wide), BF16),
            pltpu.VMEM((pieces, width, step), BF16),
            pltpu.VMEM((width, rank), BF16),
            pltpu.VMEM((total, columns), BF16),
            pltpu.VMEM((total, 2 * rank), BF16),
            pltpu.SemaphoreType.DMA((fetched,)),
            pltpu.SemaphoreType.DMA((pieces,)),
            pltpu.SemaphoreType.DMA,
            pltpu.SemaphoreType.DMA((pieces + 1,)),
        ],
        2 * total * width * (columns + rank),
        2 * width * (columns + total + rank),
    )(ids, *units, weight, down)


def late_ranks(ids, units, places, down, early, early_places, count):
    fetched, rows = len(units), units[0].shape[0]
    wide = units[0].shape[1]
    width, rank = down.shape
    total = (len(places) + len(early_places)) * rows

    def kernel(ids, *refs):
        units, refs = refs[:fetched], refs[fetched:]
        down, early, out, held, d_held, o_held, sem, d_sem, e_sem, o_sem = refs
        copies = fetch_rows(units, held, sem) + [pltpu.make_async_copy(down, d_held, d_sem)]
        for j, place in enumerate(early_places):
            at = pl.ds(row_of(ids[0], place, count, rows), rows)
            part = early.at[pl.ds(j * rows, rows)]
            copies.append(pltpu.make_async_copy(part, o_held.at[at], e_sem.at[j]))
        start_all(copies)
        wait_all(copies)
        low = masked_ranks(ids[0], held, d_held)
        for j, place in enumerate(places):
            at = pl.ds(row_of(ids[0], place, count, rows), rows)
            o_held[at] = low[j * rows : (j + 1) * rows]
        copies = [pltpu.make_async_copy(o_held, out.at[i], o_sem.at[i]) for i in range(count)]
        start_all(copies)
        wait_all(copies)

    return call(
        kernel,
        [(count, total, 2 * rank)],
        [SMEM] + [HBM] * (fetched + 2),
        [
            pltpu.VMEM((fetched * rows, wide), BF16),
            pltpu.VMEM((width, rank), BF16),
            pltpu.VMEM((total, 2 * rank), BF16),
            pltpu.SemaphoreType.DMA((fetched,)),
            pltpu.SemaphoreType.DMA,
            pltpu.SemaphoreType.DMA((len(early_places),)),
            pltpu.SemaphoreType.DMA((count,)),
        ],
        2 * fetched * rows * width * rank,
        2 * width * (fetched * rows + rank),
    )(ids, *units, down, early)[0]


def base_rows(ids, units, weight):
    fetched, rows = len(units), units[0].shape[0]
    wide = units[0].shape[1]
    width, columns = weight.shape
    total = fetched * rows
    step = min(512, columns)
    pieces = columns // step

    def kernel(ids, *refs):
        units, refs = refs[:fetched], refs[fetched:]
        weight, out, held, w_held, o_held, sem, w_sem, o_sem = refs
        x_copies = fetch_rows(units, held, sem)
        w_copies, o_copies = [], []
        for i in range(pieces):
            at = pl.ds(i * step, step)
            w_copies.append(pltpu.make_async_copy(weight.at[:, at], w_held.at[i], w_sem.at[i]))
            o_copies.append(pltpu.make_async_copy(o_held.at[:, at], out.at[:, at], o_sem.at[i]))
        start_all(x_copies)
        start_all(w_copies)
        wait_all(x_copies)
        for i in range(pieces):
            w_copies[i].wait()
            o_held[:, i * step : (i + 1) * step] = jnp.dot(
                held[:, :width], w_held[i], preferred_element_type=F32
            ).astype(BF16)
            o_copies[i].start()
        wait_all(o_copies)

    return call(
        kernel,
        [(total, columns)],
        [SMEM] + [HBM] * (fetched + 1),
        [
            pltpu.VMEM((total, wide), BF16),
            pltpu.VMEM((pieces, width, step), BF16),
            pltpu.VMEM((total, columns), BF16),
            pltpu.SemaphoreType.DMA((fetched,)),
            pltpu.SemaphoreType.DMA((pieces,)),
            pltpu.SemaphoreType.DMA((pieces,)),
        ],
        2 * total * width * columns,
        2 * width * (columns + total),
    )(ids, *units, weight)[0]


def add_delta(ids, ups, crossed, bases, places, low):
    shares, parts = len(ups), len(bases)
    count, sub, columns = ups[0].shape
    rank = sub * shares
    total = low.shape[1]
    rows = total // len(places)
    own = total // count
    per = [base.shape[0] // rows for base in bases]

    def kernel(ids, *refs):
        ups, bases, low = refs[:shares], refs[shares : shares + parts], refs[shares + parts]
        outs = refs[shares + parts + 1 : shares + parts + 1 + count]
        u_held, b_held, o_held, l_held, sem, b_sem, l_sem, o_sem = refs[shares + parts + 1 + count :]
        l_copy = pltpu.make_async_copy(low, l_held, l_sem)
        l_copy.start()
        u_copies, b_copies = [], []
        for j, up in enumerate(ups):
            at = pl.multiple_of((ids[1] ^ crossed[j]) * sub, sub)
            u_copies.append(pltpu.make_async_copy(up, u_held.at[:, pl.ds(at, sub)], sem.at[j]))
        pieces = [(base, j) for base, units in zip(bases, per) for j in range(units)]
        for j, (base, k) in enumerate(pieces):
            at = pl.ds(row_of(ids[0], places[j], count, rows), rows)
            part = base.at[pl.ds(k * rows, rows)]
            b_copies.append(pltpu.make_async_copy(part, b_held.at[at], b_sem.at[j]))
        start_all(u_copies)
        start_all(b_copies)
        l_copy.wait()
        wide = jnp.concatenate([l_held[s][:, :rank] for s in range(count)], axis=1)
        wait_all(u_copies)
        ups_here = u_held[...].reshape(count * rank, columns)
        delta = jnp.dot(wide, ups_here, preferred_element_type=F32).astype(BF16)
        wait_all(b_copies)
        o_held[...] = (b_held[...].astype(F32) + delta.astype(F32)).astype(BF16)
        o_copies = []
        for i in range(count):
            at = pl.ds(pl.multiple_of((ids[0] ^ i) * own, own), own)
            o_copies.append(pltpu.make_async_copy(o_held.at[at], outs[i], o_sem.at[i]))
        start_all(o_copies)
        wait_all(o_copies)

    return call(
        kernel,
        [(own, columns)] * count,
        [SMEM] + [HBM] * (shares + parts + 1),
        [
            pltpu.VMEM((count, rank, columns), BF16),
            pltpu.VMEM((total, columns), BF16),
            pltpu.VMEM((total, columns), BF16),
            pltpu.VMEM(low.shape, BF16),
            pltpu.SemaphoreType.DMA((shares,)),
            pltpu.SemaphoreType.DMA((len(places),)),
            pltpu.SemaphoreType.DMA,
            pltpu.SemaphoreType.DMA((count,)),
        ],
        2 * total * count * rank * columns,
        2 * count * rank * columns,
    )(ids, *ups, *bases, low)


def split_share(ids, up, count, sub):
    columns = up.shape[1] // count

    def kernel(ids, up, out, held, sem, o_sem):
        at = pl.ds(pl.multiple_of(ids[1] * sub, sub), sub)
        copies, o_copies = [], []
        for t in range(count):
            cols = pl.ds(t * columns, columns)
            copies.append(pltpu.make_async_copy(up.at[at, cols], held.at[t], sem.at[t]))
            o_copies.append(pltpu.make_async_copy(held.at[t], out.at[t], o_sem.at[t]))
        start_all(copies)
        for t in range(count):
            copies[t].wait()
            o_copies[t].start()
        wait_all(o_copies)

    return call(
        kernel,
        [(count, sub, columns)],
        [SMEM, HBM],
        [
            pltpu.VMEM((count, sub, columns), BF16),
            pltpu.SemaphoreType.DMA((count,)),
            pltpu.SemaphoreType.DMA((count,)),
        ],
        0,
        4 * count * sub * columns,
    )(ids, up)[0]


def join_columns(ids, parts):
    count = len(parts)
    rows, columns = parts[0].shape

    def kernel(ids, *refs):
        parts, (out, held, sem, o_sem) = refs[:count], refs[count:]
        copies, o_copies = [], []
        for i, part in enumerate(parts):
            at = pl.ds(pl.multiple_of((ids[0] ^ i) * columns, columns), columns)
            copies.append(pltpu.make_async_copy(part, held.at[i], sem.at[i]))
            o_copies.append(pltpu.make_async_copy(held.at[i], out.at[:, at], o_sem.at[i]))
        start_all(copies)
        for i in range(count):
            copies[i].wait()
            o_copies[i].start()
        wait_all(o_copies)

    return call(
        kernel,
        [(rows, count * columns)],
        [SMEM] + [HBM] * count,
        [
            pltpu.VMEM((count, rows, columns), BF16),
            pltpu.SemaphoreType.DMA((count,)),
            pltpu.SemaphoreType.DMA((count,)),
        ],
        0,
        4 * rows * count * columns,
    )(ids, *parts)[0]


def after(value, *earlier):
    return lax.optimization_barrier((value, *earlier))[0]


def body(
    token_input_rows,
    base_projection_weight,
    adapter_down_maps,
    adapter_up_maps,
    token_adapter_index,
    adapter_slot_table,
):
    count = lax.axis_size("tensor")
    groups, seqs = lax.axis_size("groups"), lax.axis_size("seq")
    me = lax.axis_index("tensor")
    rows, width = token_input_rows.shape
    half = rows // 2
    rank = adapter_up_maps.shape[1]
    group_shares = max(1, min(groups, rank // (16 * seqs)))
    sub = rank // (group_shares * seqs)
    share_index = (lax.axis_index("groups") % group_shares) * seqs + lax.axis_index("seq")
    ids = jnp.stack([me, share_index]).astype(jnp.int32)

    order = ring_order(count)
    ahead = [(order[p], order[(p + 1) % count]) for p in range(count)]
    behind = [(b, a) for a, b in ahead]

    matches = token_adapter_index[:, None] == jnp.arange(count, dtype=jnp.int32)[None, :]
    slots = jnp.sum(jnp.where(matches, adapter_slot_table[None, :], 0), axis=1)
    slots = jnp.broadcast_to(slots[:, None], (rows, LANES)).astype(BF16)
    carried = jnp.concatenate([token_input_rows, slots], axis=1)

    far = count // 2
    first, second = carried[:half], carried[half:]
    chains = [[[first], [first]], [[second], [second]]]
    for k in range(1, far + 1):
        for h in range(2):
            for way, pairs in enumerate((ahead, behind)):
                if k < far or way == h:
                    chains[h][way].append(lax.ppermute(chains[h][way][-1], "tensor", pairs))
    units, places = [], []
    for k in range(far + 1):
        for h in range(2):
            for way in range(2 if k else 1):
                if k < len(chains[h][way]):
                    units.append(chains[h][way][k])
                    places.append(((-k, k)[way], h, 2))
    early = (units[:count], places[:count])
    late = (units[count:], places[count:])

    swapped = lax.ppermute(ids, "seq", [(i, (i + 1) % seqs) for i in range(seqs)])
    share = split_share(after(ids, swapped), adapter_up_maps[0], count, sub)
    ups = [lax.all_to_all(share, "tensor", split_axis=0, concat_axis=0, tiled=True)]
    crossed = [0]
    for axis, size, shared, stride in (("groups", groups, group_shares, seqs), ("seq", seqs, seqs, 1)):
        bit = 1
        while bit < shared:
            ups += [lax.ppermute(u, axis, [(i, i ^ bit) for i in range(size)]) for u in ups]
            crossed += [c ^ (bit * stride) for c in crossed]
            bit *= 2

    down = adapter_down_maps[0]
    early_base, early_low = early_rows(ids, early[0], base_projection_weight, down)
    low = late_ranks(ids, late[0], late[1], down, early_low, early[1], count)
    low_all = lax.all_to_all(low, "tensor", split_axis=0, concat_axis=0, tiled=True)
    late_base = base_rows(after(ids, low), late[0], base_projection_weight)
    results = add_delta(
        ids, ups, crossed, [early_base, late_base], early[1] + late[1], low_all
    )
    parts = [results[0]]
    for i in range(1, count):
        parts.append(lax.ppermute(results[i], "tensor", [(t, t ^ i) for t in range(count)]))
    return join_columns(ids, parts)


def solution(mesh):
    placed = (
        P(("groups", "tensor", "seq"), None),
        P(None, "tensor"),
        P("tensor", None, None),
        P("tensor", None, None),
        P(("groups", "tensor", "seq")),
        P(),
    )
    return jax.shard_map(
        body,
        mesh=mesh,
        in_specs=placed,
        out_specs=P(("groups", "tensor", "seq"), None),
        check_vma=False,
    )
```

```python
import functools

import jax
import jax.numpy as jnp
from jax import lax
from jax.experimental import pallas as pl
from jax.experimental.pallas import tpu as pltpu
from jax.sharding import PartitionSpec as P

BF16 = jnp.bfloat16
F32 = jnp.float32
HBM = pl.BlockSpec(memory_space=pltpu.HBM)
SMEM = pl.BlockSpec(memory_space=pltpu.SMEM)


def walks_back(count):
    return count % 2 == 0 and count <= 8


def ring_order(count):
    if walks_back(count):
        return list(range(0, count, 2)) + list(range(1, count, 2))[::-1]
    return list(range(count))


def owner_at(me, offset, count):
    if not walks_back(count):
        return lax.rem(me + offset + count, count)
    place = jnp.where(me % 2 == 0, me // 2, count - 1 - me // 2)
    place = lax.rem(place + offset + count, count)
    return jnp.where(place < count // 2, 2 * place, 2 * (count - 1 - place) + 1)


def starts_of(units):
    starts = [0]
    for unit in units:
        starts.append(starts[-1] + unit.shape[0])
    return starts


def fetch_rows(units, held, sem):
    starts = starts_of(units)
    return [
        pltpu.make_async_copy(unit, held.at[pl.ds(starts[j], unit.shape[0])], sem.at[j])
        for j, unit in enumerate(units)
    ]


def row_of(me, place, count, rows):
    offset, part, parts = place
    return pl.multiple_of((owner_at(me, offset, count) * parts + part) * rows, rows)


def start_all(copies):
    for copy in copies:
        copy.start()


def wait_all(copies):
    for copy in copies:
        copy.wait()


def call(kernel, outs, in_specs, scratch, flops, moved, megabytes=60):
    return pl.pallas_call(
        kernel,
        in_specs=in_specs,
        out_specs=[HBM] * len(outs),
        out_shape=[jax.ShapeDtypeStruct(out, BF16) for out in outs],
        scratch_shapes=scratch,
        compiler_params=pltpu.CompilerParams(vmem_limit_bytes=megabytes << 20),
        cost_estimate=pl.CostEstimate(flops=flops, bytes_accessed=moved, transcendentals=0),
    )


def low_ranks(held, d_held):
    low = jnp.dot(held[...], d_held[...], preferred_element_type=F32)
    return jnp.concatenate([low, jnp.zeros_like(low)], axis=1).astype(BF16)


def stream_product(held, weight, w_held, w_sem):
    bands, depth, _ = w_held.shape
    total = None
    for i in range(bands):
        band_copy(weight, w_held, w_sem, i).wait()
        part = jnp.dot(held[:, i * depth : (i + 1) * depth], w_held[i], preferred_element_type=F32)
        total = part if total is None else total + part
    return total.astype(BF16)


def start_bands(copies, weight, w_held, w_sem):
    start_all(copies)
    for i in range(w_held.shape[0]):
        if i == 2:
            wait_all(copies)
        band_copy(weight, w_held, w_sem, i).start()


def band_copy(weight, w_held, w_sem, i):
    depth = w_held.shape[1]
    return pltpu.make_async_copy(weight.at[pl.ds(i * depth, depth)], w_held.at[i], w_sem.at[i])


def early_rows(ids, units, weight, down):
    fetched, total = len(units), starts_of(units)[-1]
    wide = units[0].shape[1]
    columns = weight.shape[1]
    width, rank = down.shape
    bands = 16

    def kernel(ids, *refs):
        units, refs = refs[:fetched], refs[fetched:]
        weight, down, out, low, held, w_held, d_held, o_held, l_held, sem, w_sem, d_sem, o_sem = refs
        copies = fetch_rows(units, held, sem) + [pltpu.make_async_copy(down, d_held, d_sem)]
        o_copies = [
            pltpu.make_async_copy(l_held, low, o_sem.at[0]),
            pltpu.make_async_copy(o_held, out, o_sem.at[1]),
        ]
        start_bands(copies, weight, w_held, w_sem)
        l_held[...] = low_ranks(held, d_held)
        o_copies[0].start()
        o_held[...] = stream_product(held, weight, w_held, w_sem)
        o_copies[1].start()
        wait_all(o_copies)

    return call(
        kernel,
        [(total, columns), (total, 2 * rank)],
        [SMEM] + [HBM] * (fetched + 2),
        [
            pltpu.VMEM((total, wide), BF16),
            pltpu.VMEM((bands, width // bands, columns), BF16),
            pltpu.VMEM((width, rank), BF16),
            pltpu.VMEM((total, columns), BF16),
            pltpu.VMEM((total, 2 * rank), BF16),
            pltpu.SemaphoreType.DMA((fetched,)),
            pltpu.SemaphoreType.DMA((bands,)),
            pltpu.SemaphoreType.DMA,
            pltpu.SemaphoreType.DMA((2,)),
        ],
        2 * total * width * (columns + rank),
        2 * width * (columns + total + rank),
    )(ids, *units, weight, down)


def late_ranks(ids, units, places, down, early, early_places, slots, count):
    fetched, fresh = len(units), starts_of(units)[-1]
    wide = units[0].shape[1]
    width, rank = down.shape
    total = fresh + early.shape[0]
    rows = early.shape[0] // len(early_places)

    def kernel(ids, *refs):
        units, refs = refs[:fetched], refs[fetched:]
        down, early, slots, out, held, d_held, o_held, s_held, sem, d_sem, e_sem, s_sem, o_sem = refs
        copies = fetch_rows(units, held, sem) + [pltpu.make_async_copy(down, d_held, d_sem)]
        for j, place in enumerate(early_places):
            at = pl.ds(row_of(ids[0], place, count, rows), rows)
            part = early.at[pl.ds(j * rows, rows)]
            copies.append(pltpu.make_async_copy(part, o_held.at[at], e_sem.at[j]))
        copies.append(pltpu.make_async_copy(slots, s_held, s_sem))
        start_all(copies)
        wait_all(copies)
        low = low_ranks(held, d_held)
        starts = starts_of(units)
        for j, place in enumerate(places):
            size = units[j].shape[0]
            at = pl.ds(row_of(ids[0], place, count, size), size)
            o_held[at] = low[starts[j] : starts[j + 1]]
        own = total // count
        at = pl.ds(pl.multiple_of(ids[0] * own, own), own)
        o_held[at, rank:] = s_held[:, rank:]
        copies = [pltpu.make_async_copy(o_held, out.at[i], o_sem.at[i]) for i in range(count)]
        start_all(copies)
        wait_all(copies)

    return call(
        kernel,
        [(count, total, 2 * rank)],
        [SMEM] + [HBM] * (fetched + 3),
        [
            pltpu.VMEM((fresh, wide), BF16),
            pltpu.VMEM((width, rank), BF16),
            pltpu.VMEM((total, 2 * rank), BF16),
            pltpu.VMEM(slots.shape, BF16),
            pltpu.SemaphoreType.DMA((fetched,)),
            pltpu.SemaphoreType.DMA,
            pltpu.SemaphoreType.DMA((len(early_places),)),
            pltpu.SemaphoreType.DMA,
            pltpu.SemaphoreType.DMA((count,)),
        ],
        2 * fresh * width * rank,
        2 * width * (fresh + rank),
    )(ids, *units, down, early, slots)[0]


def base_rows(ids, units, weight):
    fetched, total = len(units), starts_of(units)[-1]
    wide = units[0].shape[1]
    width, columns = weight.shape
    bands = 16

    def kernel(ids, *refs):
        units, refs = refs[:fetched], refs[fetched:]
        weight, out, held, w_held, o_held, sem, w_sem, o_sem = refs
        start_bands(fetch_rows(units, held, sem), weight, w_held, w_sem)
        o_held[...] = stream_product(held, weight, w_held, w_sem)
        copy = pltpu.make_async_copy(o_held, out, o_sem)
        copy.start()
        copy.wait()

    return call(
        kernel,
        [(total, columns)],
        [SMEM] + [HBM] * (fetched + 1),
        [
            pltpu.VMEM((total, wide), BF16),
            pltpu.VMEM((bands, width // bands, columns), BF16),
            pltpu.VMEM((total, columns), BF16),
            pltpu.SemaphoreType.DMA((fetched,)),
            pltpu.SemaphoreType.DMA((bands,)),
            pltpu.SemaphoreType.DMA,
        ],
        2 * total * width * columns,
        2 * width * (columns + total),
    )(ids, *units, weight)[0]


def add_delta(ids, ups, crossed, pieces, low):
    bases = list({id(piece[0]): piece[0] for piece in pieces}.values())
    shares, parts = len(ups), len(bases)
    count, sub, columns = ups[0].shape
    rank = sub * shares
    total = low.shape[1]
    own = total // count
    step = min(512, columns)

    def kernel(ids, *refs):
        ups, base_refs, low = refs[:shares], refs[shares : shares + parts], refs[shares + parts]
        outs = refs[shares + parts + 1 : shares + parts + 1 + count]
        u_held, b_held, l_held, sem, b_sem, l_sem, o_sem = refs[shares + parts + 1 + count :]
        l_copy = pltpu.make_async_copy(low, l_held, l_sem)
        l_copy.start()
        u_copies, b_copies = [], []
        for j, up in enumerate(ups):
            at = pl.multiple_of((ids[1] ^ crossed[j]) * sub, sub)
            u_copies.append(pltpu.make_async_copy(up, u_held.at[:, pl.ds(at, sub)], sem.at[j]))
        for j, (base, begin, size, place) in enumerate(pieces):
            base_ref = base_refs[[b is base for b in bases].index(True)]
            at = pl.ds(row_of(ids[0], place, count, size), size)
            part = base_ref.at[pl.ds(begin, size)]
            b_copies.append(pltpu.make_async_copy(part, b_held.at[at], b_sem.at[j]))
        start_all(u_copies)
        start_all(b_copies)
        l_copy.wait()
        slots = jnp.concatenate(
            [l_held[s, s * own : (s + 1) * own, rank:] for s in range(count)], axis=0
        ).astype(F32)
        wide = jnp.concatenate(
            [jnp.where(slots == s, l_held[s][:, :rank].astype(F32), 0.0) for s in range(count)], axis=1
        ).astype(BF16)
        wait_all(u_copies)
        wait_all(b_copies)
        o_copies = []
        for n in range(0, columns, step):
            cols = slice(n, n + step)
            ups_here = u_held[:, :, cols].reshape(count * rank, step)
            delta = jnp.dot(wide, ups_here, preferred_element_type=F32).astype(BF16)
            b_held[:, cols] = (b_held[:, cols].astype(F32) + delta.astype(F32)).astype(BF16)
            for i in range(count):
                at = pl.ds(pl.multiple_of((ids[0] ^ i) * own, own), own)
                block = b_held.at[at, pl.ds(n, step)]
                o_copies.append(
                    pltpu.make_async_copy(block, outs[i].at[:, pl.ds(n, step)], o_sem.at[n // step, i])
                )
                o_copies[-1].start()
        wait_all(o_copies)

    return call(
        kernel,
        [(own, columns)] * count,
        [SMEM] + [HBM] * (shares + parts + 1),
        [
            pltpu.VMEM((count, rank, columns), BF16),
            pltpu.VMEM((total, columns), BF16),
            pltpu.VMEM(low.shape, BF16),
            pltpu.SemaphoreType.DMA((shares,)),
            pltpu.SemaphoreType.DMA((len(pieces),)),
            pltpu.SemaphoreType.DMA,
            pltpu.SemaphoreType.DMA((columns // step, count)),
        ],
        2 * total * count * rank * columns,
        2 * count * rank * columns,
    )(ids, *ups, *bases, low)


def split_share(ids, turn, up, count, sub):
    columns = up.shape[1] // count

    def kernel(ids, turn, up, out, held, sem, o_sem):
        at = pl.ds(pl.multiple_of(ids[1] * sub, sub), sub)
        copies, o_copies = [], []
        for t in range(count):
            cols = pl.ds(t * columns, columns)
            copies.append(pltpu.make_async_copy(up.at[at, cols], held.at[t], sem.at[t]))
            o_copies.append(pltpu.make_async_copy(held.at[t], out.at[t], o_sem.at[t]))
        start_all(copies)
        for t in range(count):
            copies[t].wait()
            o_copies[t].start()
        wait_all(o_copies)

    return call(
        kernel,
        [(count, sub, columns)],
        [SMEM, SMEM, HBM],
        [
            pltpu.VMEM((count, sub, columns), BF16),
            pltpu.SemaphoreType.DMA((count,)),
            pltpu.SemaphoreType.DMA((count,)),
        ],
        0,
        4 * count * sub * columns,
    )(ids, turn, up)[0]


def join_columns(ids, parts, first, whole=None):
    fetched = len(parts)
    rows, columns = parts[0].shape
    count = lax.axis_size("tensor")
    kept = [] if whole is None else [whole]

    def kernel(ids, *refs):
        parts, (out, held, sem, o_sem) = refs[:fetched], refs[fetched + len(kept) :]
        copies, o_copies = [], []
        for i, part in enumerate(parts):
            at = pl.ds(pl.multiple_of((ids[0] ^ (first + i)) * columns, columns), columns)
            copies.append(pltpu.make_async_copy(part, held.at[i], sem.at[i]))
            o_copies.append(pltpu.make_async_copy(held.at[i], out.at[:, at], o_sem.at[i]))
        start_all(copies)
        for i in range(fetched):
            copies[i].wait()
            o_copies[i].start()
        wait_all(o_copies)

    return pl.pallas_call(
        kernel,
        in_specs=[SMEM] + [HBM] * (fetched + len(kept)),
        out_specs=HBM,
        out_shape=jax.ShapeDtypeStruct((rows, count * columns), BF16),
        scratch_shapes=[
            pltpu.VMEM((fetched, rows, columns), BF16),
            pltpu.SemaphoreType.DMA((fetched,)),
            pltpu.SemaphoreType.DMA((fetched,)),
        ],
        input_output_aliases={fetched + 1: 0} if kept else {},
        compiler_params=pltpu.CompilerParams(vmem_limit_bytes=60 << 20),
    )(ids, *parts, *kept)


def after(value, *earlier):
    return lax.optimization_barrier((value, *earlier))[0]


def body(
    token_input_rows,
    base_projection_weight,
    adapter_down_maps,
    adapter_up_maps,
    token_adapter_index,
    adapter_slot_table,
):
    count = lax.axis_size("tensor")
    groups, seqs = lax.axis_size("groups"), lax.axis_size("seq")
    me = lax.axis_index("tensor")
    rows, width = token_input_rows.shape
    half = rows // 2
    rank = adapter_up_maps.shape[1]
    group_shares = max(1, min(groups, rank // (16 * seqs)))
    sub = rank // (group_shares * seqs)
    share_index = (lax.axis_index("groups") % group_shares) * seqs + lax.axis_index("seq")
    ids = jnp.stack([me, share_index]).astype(jnp.int32)

    order = ring_order(count)
    ahead = [(order[p], order[(p + 1) % count]) for p in range(count)]
    behind = [(b, a) for a, b in ahead]

    matches = token_adapter_index[:, None] == jnp.arange(count, dtype=jnp.int32)[None, :]
    slots = jnp.sum(jnp.where(matches, adapter_slot_table[None, :], 0), axis=1)
    slots = jnp.broadcast_to(slots[:, None], (rows, 2 * rank)).astype(BF16)

    far = count // 2
    down = adapter_down_maps[0]
    swapped = lax.ppermute(ids, "seq", [(i, (i + 1) % seqs) for i in range(seqs)])
    units, places = [token_input_rows], [(0, 0, 1)]
    one_way, other_way = token_input_rows, token_input_rows
    for k in range(1, far):
        one_way = lax.ppermute(one_way, "tensor", ahead)
        other_way = lax.ppermute(other_way, "tensor", behind)
        units += [one_way, other_way]
        places += [(-k, 0, 1), (k, 0, 1)]
    early = units[:far]
    early_base, early_low = early_rows(
        after(ids, *units[far - 1 : far + 1]), early, base_projection_weight, down
    )
    one_way, other_way = lax.optimization_barrier((one_way, other_way, early_low))[:2]
    units.append(lax.ppermute(one_way[:half], "tensor", ahead))
    units.append(lax.ppermute(other_way[half:], "tensor", behind))
    places += [(-far, 0, 2), (far, 1, 2)]
    late, late_places = units[far:], places[far:]

    share = split_share(ids, swapped, adapter_up_maps[0], count, sub)
    ups = [lax.all_to_all(share, "tensor", split_axis=0, concat_axis=0, tiled=True)]
    crossed = [0]
    for axis, size, shared, stride in (("groups", groups, group_shares, seqs), ("seq", seqs, seqs, 1)):
        bit = 1
        while bit < shared:
            ups += [lax.ppermute(u, axis, [(i, i ^ bit) for i in range(size)]) for u in ups]
            crossed += [c ^ (bit * stride) for c in crossed]
            bit *= 2

    low = late_ranks(ids, late, late_places, down, early_low, places[:far], slots, count)
    low_all = lax.all_to_all(low, "tensor", split_axis=0, concat_axis=0, tiled=True)
    late_base = base_rows(after(ids, low), late, base_projection_weight)
    pieces = []
    for base, held, at in ((early_base, early, places[:far]), (late_base, late, late_places)):
        starts = starts_of(held)
        for j, unit in enumerate(held):
            pieces.append((base, starts[j], unit.shape[0], at[j]))
    results = add_delta(ids, ups, crossed, pieces, low_all)
    parts = {0: results[0]}
    for i in reversed(range(1, count)):
        parts[i] = lax.ppermute(results[i], "tensor", [(t, t ^ i) for t in range(count)])
    parts = [parts[i] for i in range(count)]
    cut = 3 * count // 4
    return join_columns(ids, parts[cut:], cut, join_columns(ids, parts[:cut], 0))


def solution(mesh):
    placed = (
        P(("groups", "tensor", "seq"), None),
        P(None, "tensor"),
        P("tensor", None, None),
        P("tensor", None, None),
        P(("groups", "tensor", "seq")),
        P(),
    )
    return jax.shard_map(
        body,
        mesh=mesh,
        in_specs=placed,
        out_specs=P(("groups", "tensor", "seq"), None),
        check_vma=False,
    )
```

```python
import functools

import jax
import jax.numpy as jnp
from jax import lax
from jax.experimental import pallas as pl
from jax.experimental.pallas import tpu as pltpu
from jax.sharding import PartitionSpec as P

BF16 = jnp.bfloat16
F32 = jnp.float32
HBM = pl.BlockSpec(memory_space=pltpu.HBM)
SMEM = pl.BlockSpec(memory_space=pltpu.SMEM)
VMEM = pl.BlockSpec(memory_space=pltpu.VMEM)


def walks_back(count):
    return count % 2 == 0 and count <= 8


def ring_order(count):
    if walks_back(count):
        return list(range(0, count, 2)) + list(range(1, count, 2))[::-1]
    return list(range(count))


def owner_at(me, offset, count):
    if not walks_back(count):
        return lax.rem(me + offset + count, count)
    place = jnp.where(me % 2 == 0, me // 2, count - 1 - me // 2)
    place = lax.rem(place + offset + count, count)
    return jnp.where(place < count // 2, 2 * place, 2 * (count - 1 - place) + 1)


def starts_of(units):
    starts = [0]
    for unit in units:
        starts.append(starts[-1] + unit.shape[0])
    return starts


def fetch_rows(units, held, sem):
    starts = starts_of(units)
    return [
        pltpu.make_async_copy(unit, held.at[pl.ds(starts[j], unit.shape[0])], sem.at[j])
        for j, unit in enumerate(units)
    ]


def row_of(me, place, count, rows):
    offset, part, parts = place
    return pl.multiple_of((owner_at(me, offset, count) * parts + part) * rows, rows)


def start_all(copies):
    for copy in copies:
        copy.start()


def wait_all(copies):
    for copy in copies:
        copy.wait()


def call(kernel, outs, in_specs, scratch, flops, moved, megabytes=60):
    return pl.pallas_call(
        kernel,
        in_specs=in_specs,
        out_specs=[HBM] * len(outs),
        out_shape=[jax.ShapeDtypeStruct(out, BF16) for out in outs],
        scratch_shapes=scratch,
        compiler_params=pltpu.CompilerParams(vmem_limit_bytes=megabytes << 20),
        cost_estimate=pl.CostEstimate(flops=flops, bytes_accessed=moved, transcendentals=0),
    )


def low_ranks(held, d_held):
    low = lax.dot_general(
        held[...], d_held[...], (((1,), (1,)), ((), ())), preferred_element_type=F32
    )
    return jnp.concatenate([low, jnp.zeros_like(low)], axis=1).astype(BF16)


def stream_product(held, weight, w_held, w_sem):
    bands, depth, _ = w_held.shape
    total = None
    for i in range(bands):
        band_copy(weight, w_held, w_sem, i).wait()
        part = jnp.dot(held[:, i * depth : (i + 1) * depth], w_held[i], preferred_element_type=F32)
        total = part if total is None else total + part
    return total.astype(BF16)


def start_bands(copies, weight, w_held, w_sem):
    start_all(copies)
    for i in range(w_held.shape[0]):
        if i == 2:
            wait_all(copies)
        band_copy(weight, w_held, w_sem, i).start()


def band_copy(weight, w_held, w_sem, i):
    depth = w_held.shape[1]
    return pltpu.make_async_copy(weight.at[pl.ds(i * depth, depth)], w_held.at[i], w_sem.at[i])


def early_rows(ids, units, weight, down):
    fetched, total = len(units), starts_of(units)[-1]
    wide = units[0].shape[1]
    columns = weight.shape[1]
    rank, width = down.shape
    bands = 16

    def kernel(ids, *refs):
        units, refs = refs[:fetched], refs[fetched:]
        weight, down, out, low, held, w_held, d_held, o_held, l_held, sem, w_sem, d_sem, o_sem = refs
        copies = fetch_rows(units, held, sem) + [pltpu.make_async_copy(down, d_held, d_sem)]
        o_copies = [
            pltpu.make_async_copy(l_held, low, o_sem.at[0]),
            pltpu.make_async_copy(o_held, out, o_sem.at[1]),
        ]
        start_bands(copies, weight, w_held, w_sem)
        l_held[...] = low_ranks(held, d_held)
        o_copies[0].start()
        o_held[...] = stream_product(held, weight, w_held, w_sem)
        o_copies[1].start()
        wait_all(o_copies)

    return call(
        kernel,
        [(total, columns), (total, 2 * rank)],
        [SMEM] + [HBM] * (fetched + 2),
        [
            pltpu.VMEM((total, wide), BF16),
            pltpu.VMEM((bands, width // bands, columns), BF16),
            pltpu.VMEM((rank, width), BF16),
            pltpu.VMEM((total, columns), BF16),
            pltpu.VMEM((total, 2 * rank), BF16),
            pltpu.SemaphoreType.DMA((fetched,)),
            pltpu.SemaphoreType.DMA((bands,)),
            pltpu.SemaphoreType.DMA,
            pltpu.SemaphoreType.DMA((2,)),
        ],
        2 * total * width * (columns + rank),
        2 * width * (columns + total + rank),
        42,
    )(ids, *units, weight, down)


def late_ranks(ids, units, places, down, early, early_places, slots, count):
    fetched, fresh = len(units), starts_of(units)[-1]
    wide = units[0].shape[1]
    rank, width = down.shape
    total = fresh + early.shape[0]
    rows = early.shape[0] // len(early_places)

    def kernel(ids, *refs):
        units, refs = refs[:fetched], refs[fetched:]
        down, early, slots, out, held, d_held, o_held, s_held, sem, d_sem, e_sem, s_sem, o_sem = refs
        copies = fetch_rows(units, held, sem) + [pltpu.make_async_copy(down, d_held, d_sem)]
        for j, place in enumerate(early_places):
            at = pl.ds(row_of(ids[0], place, count, rows), rows)
            part = early.at[pl.ds(j * rows, rows)]
            copies.append(pltpu.make_async_copy(part, o_held.at[at], e_sem.at[j]))
        copies.append(pltpu.make_async_copy(slots, s_held, s_sem))
        start_all(copies)
        wait_all(copies)
        low = low_ranks(held, d_held)
        starts = starts_of(units)
        for j, place in enumerate(places):
            size = units[j].shape[0]
            at = pl.ds(row_of(ids[0], place, count, size), size)
            o_held[at] = low[starts[j] : starts[j + 1]]
        own = total // count
        at = pl.ds(pl.multiple_of(ids[0] * own, own), own)
        o_held[at, rank:] = s_held[:, rank:]
        copies = [pltpu.make_async_copy(o_held, out.at[i], o_sem.at[i]) for i in range(count)]
        start_all(copies)
        wait_all(copies)

    return call(
        kernel,
        [(count, total, 2 * rank)],
        [SMEM] + [HBM] * (fetched + 3),
        [
            pltpu.VMEM((fresh, wide), BF16),
            pltpu.VMEM((rank, width), BF16),
            pltpu.VMEM((total, 2 * rank), BF16),
            pltpu.VMEM(slots.shape, BF16),
            pltpu.SemaphoreType.DMA((fetched,)),
            pltpu.SemaphoreType.DMA,
            pltpu.SemaphoreType.DMA((len(early_places),)),
            pltpu.SemaphoreType.DMA,
            pltpu.SemaphoreType.DMA((count,)),
        ],
        2 * fresh * width * rank,
        2 * width * (fresh + rank),
        16,
    )(ids, *units, down, early, slots)[0]


def base_rows(ids, units, weight):
    fetched, total = len(units), starts_of(units)[-1]
    wide = units[0].shape[1]
    width, columns = weight.shape
    bands = 16

    def kernel(ids, *refs):
        units, refs = refs[:fetched], refs[fetched:]
        weight, out, held, w_held, o_held, sem, w_sem, o_sem = refs
        start_bands(fetch_rows(units, held, sem), weight, w_held, w_sem)
        o_held[...] = stream_product(held, weight, w_held, w_sem)
        copy = pltpu.make_async_copy(o_held, out, o_sem)
        copy.start()
        copy.wait()

    return call(
        kernel,
        [(total, columns)],
        [SMEM] + [HBM] * (fetched + 1),
        [
            pltpu.VMEM((total, wide), BF16),
            pltpu.VMEM((bands, width // bands, columns), BF16),
            pltpu.VMEM((total, columns), BF16),
            pltpu.SemaphoreType.DMA((fetched,)),
            pltpu.SemaphoreType.DMA((bands,)),
            pltpu.SemaphoreType.DMA,
        ],
        2 * total * width * columns,
        2 * width * (columns + total),
        40,
    )(ids, *units, weight)[0]


def add_delta(ids, ups, crossed, pieces, low, cuts):
    bases = list({id(piece[0]): piece[0] for piece in pieces}.values())
    shares, parts = len(ups), len(bases)
    count, sub, columns = ups[0].shape
    rank = sub * shares
    total = low.shape[1]
    own = total // count
    begin, end = cuts
    blocks = end - begin
    step = min(1024, columns)

    def kernel(ids, *refs):
        ups, base_refs, low = refs[:shares], refs[shares : shares + parts], refs[shares + parts]
        outs = refs[shares + parts + 1 : shares + parts + 1 + blocks]
        u_held, b_held, l_held, k_held, p_held, sem, b_sem, l_sem, o_sem = refs[shares + parts + 1 + blocks :]
        u_copies, b_copies = [], []
        l_copy = pltpu.make_async_copy(low, l_held, l_sem)
        l_copy.start()
        for j, up in enumerate(ups):
            at = pl.multiple_of((ids[1] ^ crossed[j]) * sub, sub)
            u_copies.append(pltpu.make_async_copy(up, u_held.at[:, pl.ds(at, sub)], sem.at[j]))
        for j, (base, row, size, place) in enumerate(pieces):
            base_ref = base_refs[[b is base for b in bases].index(True)]
            at = pl.ds(row_of(ids[0], place, count, size), size)
            part = base_ref.at[pl.ds(row, size)]
            b_copies.append(pltpu.make_async_copy(part, b_held.at[at], b_sem.at[j]))
        start_all(u_copies)
        start_all(b_copies)
        l_copy.wait()
        for i in range(blocks):
            owner = ids[0] ^ (begin + i)
            at = pl.ds(pl.multiple_of(owner * own, own), own)
            slots = l_held[owner, at][:, rank:].astype(F32)
            wide = [
                jnp.where(slots == s, l_held[s, at][:, :rank].astype(F32), 0.0) for s in range(count)
            ]
            k_held[i * own : (i + 1) * own] = jnp.concatenate(wide, axis=1).astype(BF16)
        wait_all(u_copies)
        wait_all(b_copies)
        o_copies = []
        for n in range(0, columns, step):
            cols = slice(n, n + step)
            ups_here = u_held[:, :, cols].reshape(count * rank, step)
            delta = jnp.dot(k_held[...], ups_here, preferred_element_type=F32).astype(BF16)
            for i in range(blocks):
                at = pl.ds(pl.multiple_of((ids[0] ^ (begin + i)) * own, own), own)
                here = slice(i * own, (i + 1) * own)
                p_held[here, cols] = (
                    b_held[at, cols].astype(F32) + delta[here].astype(F32)
                ).astype(BF16)
                block = p_held.at[pl.ds(i * own, own), pl.ds(n, step)]
                o_copies.append(
                    pltpu.make_async_copy(block, outs[i].at[:, pl.ds(n, step)], o_sem.at[n // step, i])
                )
                o_copies[-1].start()
        wait_all(o_copies)

    return call(
        kernel,
        [(own, columns)] * blocks,
        [SMEM] + [HBM] * (shares + parts + 1),
        [
            pltpu.VMEM((count, rank, columns), BF16),
            pltpu.VMEM((total, columns), BF16),
            pltpu.VMEM(low.shape, BF16),
            pltpu.VMEM((blocks * own, count * rank), BF16),
            pltpu.VMEM((blocks * own, columns), BF16),
            pltpu.SemaphoreType.DMA((shares,)),
            pltpu.SemaphoreType.DMA((len(pieces),)),
            pltpu.SemaphoreType.DMA,
            pltpu.SemaphoreType.DMA((columns // step, blocks)),
        ],
        2 * total * count * rank * columns,
        2 * count * rank * columns,
        60,
    )(ids, *ups, *bases, low)


def split_share(ids, turn, up, count, sub):
    columns = up.shape[1] // count

    def kernel(ids, turn, up, out, held, sem, o_sem):
        at = pl.ds(pl.multiple_of(ids[1] * sub, sub), sub)
        copies, o_copies = [], []
        for t in range(count):
            cols = pl.ds(t * columns, columns)
            copies.append(pltpu.make_async_copy(up.at[at, cols], held.at[t], sem.at[t]))
            o_copies.append(pltpu.make_async_copy(held.at[t], out.at[t], o_sem.at[t]))
        start_all(copies)
        for t in range(count):
            copies[t].wait()
            o_copies[t].start()
        wait_all(o_copies)

    return call(
        kernel,
        [(count, sub, columns)],
        [SMEM, SMEM, HBM],
        [
            pltpu.VMEM((count, sub, columns), BF16),
            pltpu.SemaphoreType.DMA((count,)),
            pltpu.SemaphoreType.DMA((count,)),
        ],
        0,
        4 * count * sub * columns,
        60,
    )(ids, turn, up)[0]


def join_columns(ids, parts, first, whole=None):
    fetched = len(parts)
    rows, columns = parts[0].shape
    count = lax.axis_size("tensor")
    kept = [] if whole is None else [whole]

    def kernel(ids, *refs):
        parts, (out, sem) = refs[:fetched], refs[fetched + len(kept) :]
        copies = []
        for i, part in enumerate(parts):
            at = pl.ds(pl.multiple_of((ids[0] ^ (first + i)) * columns, columns), columns)
            copies.append(pltpu.make_async_copy(part, out.at[:, at], sem.at[i]))
        start_all(copies)
        wait_all(copies)

    return pl.pallas_call(
        kernel,
        in_specs=[SMEM] + [VMEM] * fetched + [HBM] * len(kept),
        out_specs=HBM,
        out_shape=jax.ShapeDtypeStruct((rows, count * columns), BF16),
        scratch_shapes=[pltpu.SemaphoreType.DMA((fetched,))],
        input_output_aliases={fetched + 1: 0} if kept else {},
        compiler_params=pltpu.CompilerParams(vmem_limit_bytes=16 << 20),
    )(ids, *parts, *kept)


def after(value, *earlier):
    return lax.optimization_barrier((value, *earlier))[0]


def body(
    token_input_rows,
    base_projection_weight,
    adapter_down_maps,
    adapter_up_maps,
    token_adapter_index,
    adapter_slot_table,
):
    count = lax.axis_size("tensor")
    groups, seqs = lax.axis_size("groups"), lax.axis_size("seq")
    me = lax.axis_index("tensor")
    rows, width = token_input_rows.shape
    half = rows // 2
    rank = adapter_up_maps.shape[1]
    group_shares = max(1, min(groups, rank // (16 * seqs)))
    sub = rank // (group_shares * seqs)
    share_index = (lax.axis_index("groups") % group_shares) * seqs + lax.axis_index("seq")
    ids = jnp.stack([me, share_index]).astype(jnp.int32)

    order = ring_order(count)
    ahead = [(order[p], order[(p + 1) % count]) for p in range(count)]
    behind = [(b, a) for a, b in ahead]

    matches = token_adapter_index[:, None] == jnp.arange(count, dtype=jnp.int32)[None, :]
    slots = jnp.sum(jnp.where(matches, adapter_slot_table[None, :], 0), axis=1)
    slots = jnp.broadcast_to(slots[:, None], (rows, 2 * rank)).astype(BF16)

    far = count // 2
    down = adapter_down_maps[0].T
    swapped = lax.ppermute(ids, "seq", [(i, (i + 1) % seqs) for i in range(seqs)])
    units, places = [token_input_rows], [(0, 0, 1)]
    one_way, other_way = token_input_rows, token_input_rows
    for k in range(1, far):
        one_way = lax.ppermute(one_way, "tensor", ahead)
        other_way = lax.ppermute(other_way, "tensor", behind)
        units += [one_way, other_way]
        places += [(-k, 0, 1), (k, 0, 1)]
    early = units[:far]
    early_base, early_low = early_rows(
        after(ids, slots, *units[far - 1 : far + 1]), early, base_projection_weight, down
    )
    one_way, other_way = lax.optimization_barrier((one_way, other_way, early_low))[:2]
    units.append(lax.ppermute(one_way[:half], "tensor", ahead))
    units.append(lax.ppermute(other_way[half:], "tensor", behind))
    places += [(-far, 0, 2), (far, 1, 2)]
    late, late_places = units[far:], places[far:]

    share = split_share(ids, swapped, adapter_up_maps[0], count, sub)
    ups = [lax.all_to_all(share, "tensor", split_axis=0, concat_axis=0, tiled=True)]
    crossed = [0]
    for axis, size, shared, stride in (("groups", groups, group_shares, seqs), ("seq", seqs, seqs, 1)):
        bit = 1
        while bit < shared:
            ups += [lax.ppermute(u, axis, [(i, i ^ bit) for i in range(size)]) for u in ups]
            crossed += [c ^ (bit * stride) for c in crossed]
            bit *= 2

    low = late_ranks(ids, late, late_places, down, early_low, places[:far], slots, count)
    low_all = lax.all_to_all(low, "tensor", split_axis=0, concat_axis=0, tiled=True)
    late_base = base_rows(after(ids, low), late, base_projection_weight)
    pieces = []
    for base, held, at in ((early_base, early, places[:far]), (late_base, late, late_places)):
        starts = starts_of(held)
        for j, unit in enumerate(held):
            pieces.append((base, starts[j], unit.shape[0], at[j]))
    parts = list(add_delta(ids, ups, crossed, pieces, low_all, (0, count)))
    for i in reversed(range(1, count)):
        parts[i] = lax.ppermute(parts[i], "tensor", [(t, t ^ i) for t in range(count)])
    cut = 3 * count // 4
    return join_columns(ids, parts[cut:], cut, join_columns(ids, parts[:cut], 0))


def solution(mesh):
    placed = (
        P(("groups", "tensor", "seq"), None),
        P(None, "tensor"),
        P("tensor", None, None),
        P("tensor", None, None),
        P(("groups", "tensor", "seq")),
        P(),
    )
    return jax.shard_map(
        body,
        mesh=mesh,
        in_specs=placed,
        out_specs=P(("groups", "tensor", "seq"), None),
        check_vma=False,
    )
```

```python
import functools

import jax
import jax.numpy as jnp
from jax import lax
from jax.experimental import pallas as pl
from jax.experimental.pallas import tpu as pltpu
from jax.sharding import PartitionSpec as P

BF16 = jnp.bfloat16
F32 = jnp.float32
HBM = pl.BlockSpec(memory_space=pltpu.HBM)
SMEM = pl.BlockSpec(memory_space=pltpu.SMEM)
VMEM = pl.BlockSpec(memory_space=pltpu.VMEM)


def walks_back(count):
    return count % 2 == 0 and count <= 8


def ring_order(count):
    if walks_back(count):
        return list(range(0, count, 2)) + list(range(1, count, 2))[::-1]
    return list(range(count))


def owner_at(me, offset, count):
    if not walks_back(count):
        return lax.rem(me + offset + count, count)
    place = jnp.where(me % 2 == 0, me // 2, count - 1 - me // 2)
    place = lax.rem(place + offset + count, count)
    return jnp.where(place < count // 2, 2 * place, 2 * (count - 1 - place) + 1)


def starts_of(units):
    starts = [0]
    for unit in units:
        starts.append(starts[-1] + unit.shape[0])
    return starts


def fetch_rows(units, held, sem):
    starts = starts_of(units)
    return [
        pltpu.make_async_copy(unit, held.at[pl.ds(starts[j], unit.shape[0])], sem.at[j])
        for j, unit in enumerate(units)
    ]


def row_of(me, place, count, rows):
    offset, part, parts = place
    return pl.multiple_of((owner_at(me, offset, count) * parts + part) * rows, rows)


def start_all(copies):
    for copy in copies:
        copy.start()


def wait_all(copies):
    for copy in copies:
        copy.wait()


def call(kernel, outs, in_specs, scratch, flops, moved, megabytes=60):
    return pl.pallas_call(
        kernel,
        in_specs=in_specs,
        out_specs=[HBM] * len(outs),
        out_shape=[jax.ShapeDtypeStruct(out, BF16) for out in outs],
        scratch_shapes=scratch,
        compiler_params=pltpu.CompilerParams(vmem_limit_bytes=megabytes << 20),
        cost_estimate=pl.CostEstimate(flops=flops, bytes_accessed=moved, transcendentals=0),
    )


def low_ranks(held, d_held):
    low = lax.dot_general(
        held[...], d_held[...], (((1,), (1,)), ((), ())), preferred_element_type=F32
    )
    return jnp.concatenate([low, jnp.zeros_like(low)], axis=1).astype(BF16)


def stream_product(held, weight, w_held, w_sem):
    bands, depth, _ = w_held.shape
    total = None
    for i in range(bands):
        band_copy(weight, w_held, w_sem, i).wait()
        part = jnp.dot(held[:, i * depth : (i + 1) * depth], w_held[i], preferred_element_type=F32)
        total = part if total is None else total + part
    return total.astype(BF16)


def start_bands(copies, weight, w_held, w_sem):
    start_all(copies)
    for i in range(w_held.shape[0]):
        if i == 2:
            wait_all(copies)
        band_copy(weight, w_held, w_sem, i).start()


def band_copy(weight, w_held, w_sem, i):
    depth = w_held.shape[1]
    return pltpu.make_async_copy(weight.at[pl.ds(i * depth, depth)], w_held.at[i], w_sem.at[i])


def early_rows(ids, units, weight, down):
    fetched, total = len(units), starts_of(units)[-1]
    wide = units[0].shape[1]
    columns = weight.shape[1]
    rank, width = down.shape
    bands = 16

    def kernel(ids, *refs):
        units, refs = refs[:fetched], refs[fetched:]
        weight, down, out, low, held, w_held, d_held, o_held, l_held, sem, w_sem, d_sem, o_sem = refs
        copies = fetch_rows(units, held, sem) + [pltpu.make_async_copy(down, d_held, d_sem)]
        o_copies = [
            pltpu.make_async_copy(l_held, low, o_sem.at[0]),
            pltpu.make_async_copy(o_held, out, o_sem.at[1]),
        ]
        start_bands(copies, weight, w_held, w_sem)
        l_held[...] = low_ranks(held, d_held)
        o_copies[0].start()
        o_held[...] = stream_product(held, weight, w_held, w_sem)
        o_copies[1].start()
        wait_all(o_copies)

    return call(
        kernel,
        [(total, columns), (total, 2 * rank)],
        [SMEM] + [HBM] * (fetched + 2),
        [
            pltpu.VMEM((total, wide), BF16),
            pltpu.VMEM((bands, width // bands, columns), BF16),
            pltpu.VMEM((rank, width), BF16),
            pltpu.VMEM((total, columns), BF16),
            pltpu.VMEM((total, 2 * rank), BF16),
            pltpu.SemaphoreType.DMA((fetched,)),
            pltpu.SemaphoreType.DMA((bands,)),
            pltpu.SemaphoreType.DMA,
            pltpu.SemaphoreType.DMA((2,)),
        ],
        2 * total * width * (columns + rank),
        2 * width * (columns + total + rank),
        42,
    )(ids, *units, weight, down)


def late_ranks(ids, units, places, down, early, early_places, slots, count):
    fetched, fresh = len(units), starts_of(units)[-1]
    wide = units[0].shape[1]
    rank, width = down.shape
    total = fresh + early.shape[0]
    rows = early.shape[0] // len(early_places)

    def kernel(ids, *refs):
        units, refs = refs[:fetched], refs[fetched:]
        down, early, slots, out, held, d_held, o_held, s_held, sem, d_sem, e_sem, s_sem, o_sem = refs
        copies = fetch_rows(units, held, sem) + [pltpu.make_async_copy(down, d_held, d_sem)]
        for j, place in enumerate(early_places):
            at = pl.ds(row_of(ids[0], place, count, rows), rows)
            part = early.at[pl.ds(j * rows, rows)]
            copies.append(pltpu.make_async_copy(part, o_held.at[at], e_sem.at[j]))
        copies.append(pltpu.make_async_copy(slots, s_held, s_sem))
        start_all(copies)
        wait_all(copies)
        low = low_ranks(held, d_held)
        starts = starts_of(units)
        for j, place in enumerate(places):
            size = units[j].shape[0]
            at = pl.ds(row_of(ids[0], place, count, size), size)
            o_held[at] = low[starts[j] : starts[j + 1]]
        own = total // count
        at = pl.ds(pl.multiple_of(ids[0] * own, own), own)
        o_held[at, rank:] = s_held[:, rank:]
        copies = [pltpu.make_async_copy(o_held, out.at[i], o_sem.at[i]) for i in range(count)]
        start_all(copies)
        wait_all(copies)

    return call(
        kernel,
        [(count, total, 2 * rank)],
        [SMEM] + [HBM] * (fetched + 3),
        [
            pltpu.VMEM((fresh, wide), BF16),
            pltpu.VMEM((rank, width), BF16),
            pltpu.VMEM((total, 2 * rank), BF16),
            pltpu.VMEM(slots.shape, BF16),
            pltpu.SemaphoreType.DMA((fetched,)),
            pltpu.SemaphoreType.DMA,
            pltpu.SemaphoreType.DMA((len(early_places),)),
            pltpu.SemaphoreType.DMA,
            pltpu.SemaphoreType.DMA((count,)),
        ],
        2 * fresh * width * rank,
        2 * width * (fresh + rank),
        16,
    )(ids, *units, down, early, slots)[0]


def base_rows(ids, units, weight):
    fetched, total = len(units), starts_of(units)[-1]
    wide = units[0].shape[1]
    width, columns = weight.shape
    bands = 16

    def kernel(ids, *refs):
        units, refs = refs[:fetched], refs[fetched:]
        weight, out, held, w_held, o_held, sem, w_sem, o_sem = refs
        start_bands(fetch_rows(units, held, sem), weight, w_held, w_sem)
        o_held[...] = stream_product(held, weight, w_held, w_sem)
        copy = pltpu.make_async_copy(o_held, out, o_sem)
        copy.start()
        copy.wait()

    return call(
        kernel,
        [(total, columns)],
        [SMEM] + [HBM] * (fetched + 1),
        [
            pltpu.VMEM((total, wide), BF16),
            pltpu.VMEM((bands, width // bands, columns), BF16),
            pltpu.VMEM((total, columns), BF16),
            pltpu.SemaphoreType.DMA((fetched,)),
            pltpu.SemaphoreType.DMA((bands,)),
            pltpu.SemaphoreType.DMA,
        ],
        2 * total * width * columns,
        2 * width * (columns + total),
        40,
    )(ids, *units, weight)[0]


def add_delta(ids, ups, crossed, pieces, low, cuts):
    bases = list({id(piece[0]): piece[0] for piece in pieces}.values())
    shares, parts = len(ups), len(bases)
    count, sub, columns = ups[0].shape
    rank = sub * shares
    total = low.shape[1]
    own = total // count
    begin, end = cuts
    blocks = end - begin
    step = min(1024, columns)

    def kernel(ids, *refs):
        ups, base_refs, low = refs[:shares], refs[shares : shares + parts], refs[shares + parts]
        outs = refs[shares + parts + 1 : shares + parts + 1 + blocks]
        u_held, b_held, l_held, k_held, p_held, sem, b_sem, l_sem, o_sem = refs[shares + parts + 1 + blocks :]
        u_copies, b_copies = [], []
        l_copy = pltpu.make_async_copy(low, l_held, l_sem)
        l_copy.start()
        for j, up in enumerate(ups):
            at = pl.multiple_of((ids[1] ^ crossed[j]) * sub, sub)
            u_copies.append(pltpu.make_async_copy(up, u_held.at[:, pl.ds(at, sub)], sem.at[j]))
        for j, (base, row, size, place) in enumerate(pieces):
            base_ref = base_refs[[b is base for b in bases].index(True)]
            at = pl.ds(row_of(ids[0], place, count, size), size)
            part = base_ref.at[pl.ds(row, size)]
            b_copies.append(pltpu.make_async_copy(part, b_held.at[at], b_sem.at[j]))
        start_all(u_copies)
        start_all(b_copies)
        l_copy.wait()
        for i in range(blocks):
            owner = ids[0] ^ (begin + i)
            at = pl.ds(pl.multiple_of(owner * own, own), own)
            slots = l_held[owner, at][:, rank:].astype(F32)
            wide = [
                jnp.where(slots == s, l_held[s, at][:, :rank].astype(F32), 0.0) for s in range(count)
            ]
            k_held[i * own : (i + 1) * own] = jnp.concatenate(wide, axis=1).astype(BF16)
        wait_all(u_copies)
        wait_all(b_copies)
        o_copies = []
        for n in range(0, columns, step):
            cols = slice(n, n + step)
            ups_here = u_held[:, :, cols].reshape(count * rank, step)
            delta = jnp.dot(k_held[...], ups_here, preferred_element_type=F32).astype(BF16)
            for i in range(blocks):
                at = pl.ds(pl.multiple_of((ids[0] ^ (begin + i)) * own, own), own)
                here = slice(i * own, (i + 1) * own)
                p_held[here, cols] = (
                    b_held[at, cols].astype(F32) + delta[here].astype(F32)
                ).astype(BF16)
                block = p_held.at[pl.ds(i * own, own), pl.ds(n, step)]
                o_copies.append(
                    pltpu.make_async_copy(block, outs[i].at[:, pl.ds(n, step)], o_sem.at[n // step, i])
                )
                o_copies[-1].start()
        wait_all(o_copies)

    return call(
        kernel,
        [(own, columns)] * blocks,
        [SMEM] + [HBM] * (shares + parts) + [VMEM],
        [
            pltpu.VMEM((count, rank, columns), BF16),
            pltpu.VMEM((total, columns), BF16),
            pltpu.VMEM(low.shape, BF16),
            pltpu.VMEM((blocks * own, count * rank), BF16),
            pltpu.VMEM((blocks * own, columns), BF16),
            pltpu.SemaphoreType.DMA((shares,)),
            pltpu.SemaphoreType.DMA((len(pieces),)),
            pltpu.SemaphoreType.DMA,
            pltpu.SemaphoreType.DMA((columns // step, blocks)),
        ],
        2 * total * count * rank * columns,
        2 * count * rank * columns,
        60,
    )(ids, *ups, *bases, low)


def split_share(ids, turn, up, count, sub):
    columns = up.shape[1] // count

    def kernel(ids, turn, up, out, held, sem, o_sem):
        at = pl.ds(pl.multiple_of(ids[1] * sub, sub), sub)
        copies, o_copies = [], []
        for t in range(count):
            cols = pl.ds(t * columns, columns)
            copies.append(pltpu.make_async_copy(up.at[at, cols], held.at[t], sem.at[t]))
            o_copies.append(pltpu.make_async_copy(held.at[t], out.at[t], o_sem.at[t]))
        start_all(copies)
        for t in range(count):
            copies[t].wait()
            o_copies[t].start()
        wait_all(o_copies)

    return call(
        kernel,
        [(count, sub, columns)],
        [SMEM, SMEM, HBM],
        [
            pltpu.VMEM((count, sub, columns), BF16),
            pltpu.SemaphoreType.DMA((count,)),
            pltpu.SemaphoreType.DMA((count,)),
        ],
        0,
        4 * count * sub * columns,
        60,
    )(ids, turn, up)[0]


def join_columns(ids, parts, first, whole=None):
    fetched = len(parts)
    rows, columns = parts[0].shape
    count = lax.axis_size("tensor")
    kept = [] if whole is None else [whole]

    def kernel(ids, *refs):
        parts, (out, sem) = refs[:fetched], refs[fetched + len(kept) :]
        copies = []
        for i, part in enumerate(parts):
            at = pl.ds(pl.multiple_of((ids[0] ^ (first + i)) * columns, columns), columns)
            copies.append(pltpu.make_async_copy(part, out.at[:, at], sem.at[i]))
        start_all(copies)
        wait_all(copies)

    return pl.pallas_call(
        kernel,
        in_specs=[SMEM] + [VMEM] * fetched + [HBM] * len(kept),
        out_specs=HBM,
        out_shape=jax.ShapeDtypeStruct((rows, count * columns), BF16),
        scratch_shapes=[pltpu.SemaphoreType.DMA((fetched,))],
        input_output_aliases={fetched + 1: 0} if kept else {},
        compiler_params=pltpu.CompilerParams(vmem_limit_bytes=16 << 20),
    )(ids, *parts, *kept)


def after(value, *earlier):
    return lax.optimization_barrier((value, *earlier))[0]


def body(
    token_input_rows,
    base_projection_weight,
    adapter_down_maps,
    adapter_up_maps,
    token_adapter_index,
    adapter_slot_table,
):
    count = lax.axis_size("tensor")
    groups, seqs = lax.axis_size("groups"), lax.axis_size("seq")
    me = lax.axis_index("tensor")
    rows, width = token_input_rows.shape
    half = rows // 2
    rank = adapter_up_maps.shape[1]
    group_shares = max(1, min(groups, rank // (16 * seqs)))
    sub = rank // (group_shares * seqs)
    share_index = (lax.axis_index("groups") % group_shares) * seqs + lax.axis_index("seq")
    ids = jnp.stack([me, share_index]).astype(jnp.int32)

    order = ring_order(count)
    ahead = [(order[p], order[(p + 1) % count]) for p in range(count)]
    behind = [(b, a) for a, b in ahead]

    matches = token_adapter_index[:, None] == jnp.arange(count, dtype=jnp.int32)[None, :]
    slots = jnp.sum(jnp.where(matches, adapter_slot_table[None, :], 0), axis=1)
    slots = jnp.broadcast_to(slots[:, None], (rows, 2 * rank)).astype(BF16)

    far = count // 2
    down = adapter_down_maps[0].T
    swapped = lax.ppermute(ids, "seq", [(i, (i + 1) % seqs) for i in range(seqs)])
    units, places = [token_input_rows], [(0, 0, 1)]
    one_way, other_way = token_input_rows, token_input_rows
    for k in range(1, far):
        one_way = lax.ppermute(one_way, "tensor", ahead)
        other_way = lax.ppermute(other_way, "tensor", behind)
        units += [one_way, other_way]
        places += [(-k, 0, 1), (k, 0, 1)]
    early = units[:far]
    early_base, early_low = early_rows(
        after(ids, slots, *units[far - 1 : far + 1]), early, base_projection_weight, down
    )
    one_way, other_way = lax.optimization_barrier((one_way, other_way, early_low))[:2]
    units.append(lax.ppermute(one_way[:half], "tensor", ahead))
    units.append(lax.ppermute(other_way[half:], "tensor", behind))
    places += [(-far, 0, 2), (far, 1, 2)]
    late, late_places = units[far:], places[far:]

    share = split_share(ids, swapped, adapter_up_maps[0], count, sub)
    ups = [lax.all_to_all(share, "tensor", split_axis=0, concat_axis=0, tiled=True)]
    crossed = [0]
    for axis, size, shared, stride in (("groups", groups, group_shares, seqs), ("seq", seqs, seqs, 1)):
        bit = 1
        while bit < shared:
            ups += [lax.ppermute(u, axis, [(i, i ^ bit) for i in range(size)]) for u in ups]
            crossed += [c ^ (bit * stride) for c in crossed]
            bit *= 2

    low = late_ranks(ids, late, late_places, down, early_low, places[:far], slots, count)
    low_all = lax.all_to_all(low, "tensor", split_axis=0, concat_axis=0, tiled=True)
    late_base = base_rows(after(ids, low), late, base_projection_weight)
    pieces = []
    for base, held, at in ((early_base, early, places[:far]), (late_base, late, late_places)):
        starts = starts_of(held)
        for j, unit in enumerate(held):
            pieces.append((base, starts[j], unit.shape[0], at[j]))
    parts = list(add_delta(ids, ups, crossed, pieces, low_all, (0, count)))
    for i in reversed(range(1, count)):
        parts[i] = lax.ppermute(parts[i], "tensor", [(t, t ^ i) for t in range(count)])
    cut = 3 * count // 4
    return join_columns(ids, parts[cut:], cut, join_columns(ids, parts[:cut], 0))


def solution(mesh):
    placed = (
        P(("groups", "tensor", "seq"), None),
        P(None, "tensor"),
        P("tensor", None, None),
        P("tensor", None, None),
        P(("groups", "tensor", "seq")),
        P(),
    )
    return jax.shard_map(
        body,
        mesh=mesh,
        in_specs=placed,
        out_specs=P(("groups", "tensor", "seq"), None),
        check_vma=False,
    )
```
